32 devices in a mesh: dp: 8 (over z, x), tensor: 4 (over y, core).
Axes of the slice: x: 2, y: 2, z: 4, core: 2. Of those that a mesh axis runs over, the one named last changes fastest.
Arguments:
- tokens: bfloat16 [2048, 8192], P('dp', 'tensor'), may hold values from -6 to 6
- key_value_weight: bfloat16 [8192, 8, 256], P('tensor'), may hold values from -0.09375 to 0.09375
- key_value_bias: bfloat16 [8, 256], P('tensor'), may hold values from -3 to 3
- adapter_down_weight: bfloat16 [16, 8192, 128], P('dp', 'tensor'), may hold values from -0.0625 to 0.0625
- adapter_up_weight: bfloat16 [16, 8, 2, 64, 128], P('dp', 'tensor'), may hold values from -0.75 to 0.75
- conversation_adapter: int32 [32], replicated, may hold values from 0 to 15, as said below
- adapter_slot_table: int32 [16], replicated, may hold values from 0 to 15, as said below
- span_length: int32 [32], P('dp'), may hold values from 40 to 64, as said below
- context_length: int32 [32], P('dp'), may hold values from 0 to 4096
Outputs:
- new_kv: bfloat16 [8, 2048, 256], P('tensor', 'dp')
The draws below stay inside these ranges and needn't reach their ends.
Inputs may be any that keep to these rules, and one draw needn't show every extreme that they name: `conversation_adapter`: the 4 conversations of each index of dp use adapters whose slots lie on 4 different owners (owner of slot p: p // 2), so an owner serves at most one conversation of each index of dp, and some owner serves one of every index. `adapter_slot_table`: A permutation: every storage slot holds exactly one adapter. `span_length`: every index of dp has a conversation whose span fills all 64 slots.
All inputs are finite; a program needn't handle non-finite values.
Results may differ from the reference program's by a relative error of at most 0.019.
Values may be sent and summed in bfloat16 or wider, within the bound.
A program may use at most 128 MiB of HBM per device.

```python
import math
import jax
import jax.numpy as jnp
from jax import lax

MODEL_WIDTH = 8192
KEY_VALUE_HEADS = 8
HEAD_SIZE = 128
ADAPTER_RANK = 64
ADP_DEV = 2
SPAN = 64
CTX = 4096
CONV_DP = 4
CONVS = 32
TOKENS = 2048
ADAPTER_COUNT = 16
N_DP = 8
N_TENSOR = 4


def routing_draw(key):
    key = jax.random.fold_in(key, 4242)
    key_perm, key_hot, key_pick, key_local = jax.random.split(key, 4)
    slot_of = jax.random.permutation(key_perm, ADP_DEV * N_DP).astype(jnp.int32)
    adapter_at = jnp.argsort(slot_of).astype(jnp.int32)
    hot_owner = jax.random.randint(key_hot, (), 0, N_DP).astype(jnp.int32)
    group_keys = jax.random.split(key_pick, N_DP)

    def one_group(group_key):
        key_order, key_roll = jax.random.split(group_key)
        others = jax.random.permutation(key_order, N_DP - 1).astype(jnp.int32)[:CONV_DP - 1]
        owners = jnp.concatenate([hot_owner[None], (hot_owner + 1 + others) % N_DP])
        roll_by = jax.random.randint(key_roll, (), 0, CONV_DP)
        return jnp.roll(owners, roll_by)
    owners = jax.vmap(one_group)(group_keys)
    local_pick = jax.random.randint(key_local, (N_DP, CONV_DP), 0, ADP_DEV).astype(jnp.int32)
    adapters = adapter_at[owners * ADP_DEV + local_pick]
    return (slot_of, adapters.reshape(-1).astype(jnp.int32), (owners == hot_owner).reshape(-1))


def draw_conversation_adapter(key, part):
    return routing_draw(key)[1]


def draw_adapter_slot_table(key, part):
    return routing_draw(key)[0]


def draw_span_length(key, part):
    hot_rows = routing_draw(key)[2]
    drawn = jax.random.randint(jax.random.fold_in(key, 77), (CONV_DP * N_DP,), SPAN * 5 // 8, SPAN + 1).astype(jnp.int32)
    return jnp.where(hot_rows, SPAN, drawn).astype(jnp.int32)


def touch_ends(entries, rng, least, high):
    longest = entries.shape.index(max(entries.shape))
    spots = []
    for shift in (0, 1):
        where = [jax.random.randint(jax.random.fold_in(rng, axis), (), 0, length) for axis, length in enumerate(entries.shape)]
        where[longest] = (where[longest] + shift) % entries.shape[longest]
        spots.append(tuple(where))
    return entries.at[spots[0]].set(least).at[spots[1]].set(high)


def with_spikes(entries, own_key, source, target, parts, factor):
    def block_of(dim):
        return (jnp.arange(entries.shape[dim]) // (entries.shape[dim] // parts)).reshape((-1,) + (1,) * (entries.ndim - 1 - dim))

    near = jax.random.permutation(own_key, parts)[block_of(target)]
    other_side = (block_of(target) + parts // 2) % parts
    return jnp.where((block_of(source) == near) | (block_of(source) == other_side), factor * entries, entries)


def shard_levels(own_key, extent, cuts, least, largest):
    def one(axis_at, shards_of):
        heights = jax.random.uniform(jax.random.fold_in(jax.random.fold_in(own_key, 6), axis_at), (shards_of,), jnp.float32, least / len(cuts), largest / len(cuts))
        return jnp.repeat(jnp.exp(heights), extent[axis_at] // shards_of).reshape((-1,) + (1,) * (len(extent) - axis_at - 1))

    level = one(*cuts[0])
    for cut in cuts[1:]:
        level = level * one(*cut)
    return level


def scatter_about(stream_key, dims, spread, most, cuts=(), held_as=jnp.bfloat16):
    array = spread * jax.random.normal(stream_key, dims, jnp.float32)
    if cuts:
        array = array * shard_levels(stream_key, dims, cuts, -0.22, 0.18)
    return jnp.clip(array, -most, most).astype(held_as)


def noise_with(rng, dims, deviation, limit, shards, heavy, kind=jnp.bfloat16):
    values = deviation * jax.random.normal(rng, dims, jnp.float32)
    if shards:
        values = values * shard_levels(rng, dims, shards, -0.22, 0.18)
    return jnp.clip(with_spikes(values, jax.random.fold_in(rng, 3), *heavy), -limit, limit).astype(kind)


def setup_inputs(seed: int = 0) -> dict:
    arg_keys = jax.random.split(jax.random.key(seed), 10)
    return {
        "tokens": scatter_about(arg_keys[0], (TOKENS, MODEL_WIDTH), 1.0, 6.0, ((0, 8), (1, 4))),
        "key_value_weight": noise_with(arg_keys[1], (MODEL_WIDTH, KEY_VALUE_HEADS, 2 * HEAD_SIZE), MODEL_WIDTH ** -0.5, 0.09375, ((0, 4),), (0, 1, 4, 2.0)),
        "key_value_bias": scatter_about(arg_keys[2], (KEY_VALUE_HEADS, 2 * HEAD_SIZE), 0.5, 3.0, ((0, 4),)),
        "adapter_down_weight": scatter_about(arg_keys[3], (ADAPTER_COUNT, MODEL_WIDTH, 2 * ADAPTER_RANK), MODEL_WIDTH ** -0.5, 0.0625, ((0, 8), (1, 4))),
        "adapter_up_weight": scatter_about(arg_keys[4], (ADAPTER_COUNT, KEY_VALUE_HEADS, 2, ADAPTER_RANK, HEAD_SIZE), ADAPTER_RANK ** -0.5, 0.75, ((0, 8), (1, 4))),
        "conversation_adapter": draw_conversation_adapter(jax.random.fold_in(arg_keys[9], 71), 0),
        "adapter_slot_table": draw_adapter_slot_table(jax.random.fold_in(arg_keys[9], 71), 0),
        "span_length": draw_span_length(jax.random.fold_in(arg_keys[9], 71), 0),
        "context_length": touch_ends(jax.random.randint(arg_keys[8], (CONVS,), 0, CTX + 1), jax.random.fold_in(arg_keys[8], 1), 0, CTX).astype(jnp.int32),
    }


rope_base = 1000000.0


def rotary(key_part, positions):
    half_dim = key_part.shape[-1] // 2
    inverse_freq = jnp.exp(jnp.arange(half_dim, dtype=jnp.float32) * (-2.0 * math.log(rope_base) / key_part.shape[-1]))
    angles = positions[:, None] * inverse_freq[None, :]
    angles = jnp.concatenate([angles, angles], axis=-1)
    turned = jnp.concatenate([-key_part[..., half_dim:], key_part[..., :half_dim]], axis=-1)
    return key_part * jnp.cos(angles) + turned * jnp.sin(angles)


def reference(tokens, key_value_weight, key_value_bias, adapter_down_weight, adapter_up_weight, conversation_adapter, adapter_slot_table, span_length, context_length):
    slice_width = MODEL_WIDTH // N_TENSOR
    flat_weight = key_value_weight.reshape(MODEL_WIDTH, KEY_VALUE_HEADS * 2 * HEAD_SIZE)
    base_sum = jnp.zeros((TOKENS, KEY_VALUE_HEADS * 2 * HEAD_SIZE), jnp.float32)
    for stripe in range(N_TENSOR):
        partial_sum = jnp.dot(tokens[:, stripe * slice_width:(stripe + 1) * slice_width],
                              flat_weight[stripe * slice_width:(stripe + 1) * slice_width],
                              preferred_element_type=jnp.float32)
        rounded = lax.optimization_barrier(partial_sum.astype(jnp.bfloat16))
        base_sum = base_sum + rounded.astype(jnp.float32)
    storage = adapter_slot_table[conversation_adapter].astype(jnp.int32)

    def adapt_one(item):
        conversation_rows, storage_slot_index = item
        rank_activation = jnp.dot(conversation_rows, adapter_down_weight[storage_slot_index], preferred_element_type=jnp.float32).astype(jnp.bfloat16)
        up_weight_block = adapter_up_weight[storage_slot_index].astype(jnp.float32)
        rank_halves = rank_activation.astype(jnp.float32).reshape(SPAN, 2, ADAPTER_RANK)
        adapter_delta = jnp.einsum("oiu,kiuq->okiq", rank_halves, up_weight_block)
        return adapter_delta.astype(jnp.bfloat16)

    deltas = lax.map(adapt_one, (tokens.reshape(CONVS, SPAN, MODEL_WIDTH), storage))
    projected = base_sum.reshape(TOKENS, KEY_VALUE_HEADS, 2 * HEAD_SIZE) + key_value_bias.astype(jnp.float32)[None, :, :]
    projected = projected + deltas.reshape(TOKENS, KEY_VALUE_HEADS, 2 * HEAD_SIZE).astype(jnp.float32)
    projected = jnp.transpose(projected, (1, 0, 2))
    positions = (context_length[:, None] + jnp.arange(SPAN, dtype=jnp.int32)[None, :]).reshape(TOKENS).astype(jnp.float32)
    rotated = rotary(projected[..., :HEAD_SIZE], positions)
    live_mask = (jnp.arange(SPAN, dtype=jnp.int32)[None, :] < span_length[:, None]).reshape(TOKENS)
    joined = jnp.concatenate([rotated, projected[..., HEAD_SIZE:]], axis=-1)
    return jnp.where(live_mask[None, :, None], joined, 0.0).astype(jnp.bfloat16)
```

```python
import math

import jax
import jax.numpy as jnp
from jax import lax
from jax.sharding import PartitionSpec as P

rope_base = 1000000.0


def rotary(key_part, positions):
    half_dim = key_part.shape[-1] // 2
    inverse_freq = jnp.exp(
        jnp.arange(half_dim, dtype=jnp.float32) * (-2.0 * math.log(rope_base) / key_part.shape[-1])
    )
    angles = positions[:, None] * inverse_freq[None, :]
    angles = jnp.concatenate([angles, angles], axis=-1)
    turned = jnp.concatenate([-key_part[..., half_dim:], key_part[..., :half_dim]], axis=-1)
    return key_part * jnp.cos(angles) + turned * jnp.sin(angles)


def body(
    tokens,
    key_value_weight,
    key_value_bias,
    adapter_down_weight,
    adapter_up_weight,
    conversation_adapter,
    adapter_slot_table,
    span_length,
    context_length,
):
    dp_count = lax.axis_size("dp")
    owner_index = lax.axis_index("dp")
    conversation_present = span_length.shape[0]
    span_token_rows = tokens.shape[0] // conversation_present
    slice_width = tokens.shape[1]
    heads_present = key_value_bias.shape[0]
    head_span_width = key_value_bias.shape[1]
    head_dim = head_span_width // 2
    locally_stored = adapter_down_weight.shape[0]
    double_rank = adapter_down_weight.shape[2]
    adapter_ids = jnp.arange(adapter_slot_table.shape[0], dtype=jnp.int32)
    storage = jnp.sum(
        jnp.where(
            conversation_adapter[:, None] == adapter_ids[None, :], adapter_slot_table[None, :], 0
        ),
        axis=1,
    )
    owner_table = (storage // locally_stored).reshape(dp_count, conversation_present)
    local_table = (storage % locally_stored).reshape(dp_count, conversation_present)
    my_owners = lax.dynamic_slice_in_dim(owner_table, owner_index, 1, 0)[0]
    owner_ids = jnp.arange(dp_count, dtype=jnp.int32)
    served_slot = jnp.sum(jnp.where(owner_table == owner_index, local_table, 0), axis=1)
    conversation_rows = tokens.reshape(conversation_present, span_token_rows, slice_width)
    outgoing = jnp.zeros((dp_count, span_token_rows, slice_width), tokens.dtype)
    for c in range(conversation_present):
        outgoing = jnp.where(
            (my_owners[c] == owner_ids)[:, None, None], conversation_rows[c][None], outgoing
        )
    visiting = lax.all_to_all(outgoing, "dp", split_axis=0, concat_axis=0, tiled=True)
    base_sum = lax.psum_scatter(
        jnp.einsum(
            "td,dhe->hte", tokens, key_value_weight, preferred_element_type=jnp.float32
        ).astype(jnp.bfloat16),
        "tensor",
        scatter_dimension=0,
        tiled=True,
    ).astype(jnp.float32)
    rank_each = jnp.einsum(
        "crd,sdk->scrk", visiting, adapter_down_weight, preferred_element_type=jnp.float32
    )
    rank_part = rank_each[0]
    up_served = adapter_up_weight[0][None]
    for s in range(1, locally_stored):
        rank_part = jnp.where((served_slot == s)[:, None, None], rank_each[s], rank_part)
        up_served = jnp.where(
            (served_slot == s)[:, None, None, None, None], adapter_up_weight[s][None], up_served
        )
    rank_sum = lax.psum(rank_part.astype(jnp.bfloat16), "tensor")
    rank_halves = rank_sum.reshape(dp_count, span_token_rows, 2, double_rank // 2)
    served_delta = jnp.einsum(
        "crgm,chgmf->crhgf", rank_halves, up_served, preferred_element_type=jnp.float32
    ).astype(jnp.bfloat16)
    served_delta = served_delta.reshape(
        dp_count, span_token_rows, heads_present * head_span_width
    )
    returned = lax.all_to_all(served_delta, "dp", split_axis=0, concat_axis=0, tiled=True)
    adapter_delta = jnp.zeros((conversation_present,) + returned.shape[1:], returned.dtype)
    for o in range(dp_count):
        adapter_delta = jnp.where(
            (my_owners == o)[:, None, None], returned[o][None], adapter_delta
        )
    conversation_delta = adapter_delta.reshape(
        conversation_present, span_token_rows, heads_present * head_span_width
    ).astype(jnp.float32)
    delta_heads = jnp.transpose(
        conversation_delta.reshape(
            conversation_present * span_token_rows, heads_present, head_span_width
        ),
        (1, 0, 2),
    )
    projected = base_sum + key_value_bias.astype(jnp.float32)[:, None, :] + delta_heads
    positions = (
        (context_length[:, None] + jnp.arange(span_token_rows, dtype=jnp.int32)[None, :])
        .reshape(-1)
        .astype(jnp.float32)
    )
    rotated = rotary(projected[..., :head_dim], positions)
    live_mask = (
        jnp.arange(span_token_rows, dtype=jnp.int32)[None, :] < span_length[:, None]
    ).reshape(-1)
    joined = jnp.concatenate([rotated, projected[..., head_dim:]], axis=-1)
    return jnp.where(live_mask[None, :, None], joined, 0.0).astype(jnp.bfloat16)


def solution(mesh):
    placed = (
        P("dp", "tensor"),
        P("tensor", None, None),
        P("tensor", None),
        P("dp", "tensor", None),
        P("dp", "tensor", None, None, None),
        P(),
        P(),
        P("dp"),
        P("dp"),
    )
    return jax.shard_map(
        body, mesh=mesh, in_specs=placed, out_specs=P("tensor", "dp", None), check_vma=False
    )
```

```python
import functools
import math

import jax
import jax.numpy as jnp
from jax import lax
from jax.experimental import pallas as pl
from jax.experimental.pallas import tpu as pltpu
from jax.sharding import PartitionSpec as P

rope_base = 1000000.0


def rotary(key_part, positions):
    half_dim = key_part.shape[-1] // 2
    inverse_freq = jnp.exp(
        jnp.arange(half_dim, dtype=jnp.float32) * (-2.0 * math.log(rope_base) / key_part.shape[-1])
    )
    angles = positions[:, None] * inverse_freq[None, :]
    angles = jnp.concatenate([angles, angles], axis=-1)
    turned = jnp.concatenate([-key_part[..., half_dim:], key_part[..., :half_dim]], axis=-1)
    return key_part * jnp.cos(angles) + turned * jnp.sin(angles)


def other(index, distance, count):
    total = 0
    step = 1
    while step < count:
        bit = lax.rem(index // step, 2)
        total = total + (bit if (distance // step) % 2 == 0 else 1 - bit) * step
        step *= 2
    return total


def adapter_kernel(
    dp_count,
    tensor_count,
    pick_ref,
    slot_ref,
    mine_ref,
    tokens_ref,
    down_ref,
    up_ref,
    delta_ref,
    up_wide,
    outgoing,
    visiting,
    part,
    peer,
    served,
    returned,
    token_send,
    token_recv,
    peer_send,
    peer_recv,
    delta_send,
    delta_recv,
):
    me_dp = lax.axis_index("dp")
    me_tensor = lax.axis_index("tensor")
    stored, heads = up_ref.shape[0], up_ref.shape[1]
    rank, half = up_ref.shape[3], up_ref.shape[4]
    partner = [other(me_dp, j, dp_count) for j in range(dp_count)]
    mate = [other(me_tensor, q, tensor_count) for q in range(tensor_count)]

    barrier = pltpu.get_barrier_semaphore()
    for j in range(1, dp_count):
        pl.semaphore_signal(
            barrier, inc=1, device_id={"dp": partner[j]}, device_id_type=pl.DeviceIdType.MESH
        )
    for q in range(1, tensor_count):
        pl.semaphore_signal(
            barrier, inc=1, device_id={"tensor": mate[q]}, device_id_type=pl.DeviceIdType.MESH
        )

    def token_copy(j):
        return pltpu.make_async_remote_copy(
            src_ref=outgoing.at[j - 1],
            dst_ref=visiting.at[j - 1],
            send_sem=token_send.at[j - 1],
            recv_sem=token_recv.at[j - 1],
            device_id={"dp": partner[j]},
            device_id_type=pl.DeviceIdType.MESH,
        )

    def peer_copy(j, q):
        return pltpu.make_async_remote_copy(
            src_ref=part.at[j],
            dst_ref=peer.at[j, q - 1],
            send_sem=peer_send.at[j, q - 1],
            recv_sem=peer_recv.at[j, q - 1],
            device_id={"tensor": mate[q]},
            device_id_type=pl.DeviceIdType.MESH,
        )

    def delta_copy(j):
        return pltpu.make_async_remote_copy(
            src_ref=served.at[j - 1],
            dst_ref=returned.at[j],
            send_sem=delta_send.at[j - 1],
            recv_sem=delta_recv.at[j - 1],
            device_id={"dp": partner[j]},
            device_id_type=pl.DeviceIdType.MESH,
        )

    def fill(j):
        outgoing[j - 1] = tokens_ref[pick_ref[j]]

    far = list(range(dp_count - 1, dp_count // 2 - 1, -1))
    near = list(range(dp_count // 2 - 1, 0, -1))
    first = far[:2] + near[:1]
    for j in first:
        fill(j)
    pl.semaphore_wait(barrier, dp_count + tensor_count - 2)
    for j in first:
        token_copy(j).start()
    far_waiting, near_waiting = far[2:], near[1:]
    for j in far_waiting + near_waiting:
        fill(j)

    up_wide[...] = jnp.zeros_like(up_wide)
    for s in range(stored):
        for h in range(heads):
            for g in range(2):
                at = (2 * h + g) * half
                up_wide[s, g * rank : (g + 1) * rank, at : at + half] = up_ref[s, h, g]

    def down_stage(j):
        if j == 0:
            rows = tokens_ref[pick_ref[0]]
        else:
            token_copy(j).wait_recv()
            rows = visiting[j - 1]
        part[j] = jnp.dot(
            rows, down_ref[slot_ref[j]], preferred_element_type=jnp.float32
        ).astype(jnp.bfloat16)
        for q in range(1, tensor_count):
            peer_copy(j, q).start()

    def up_stage(j):
        total = part[j].astype(jnp.float32)
        for q in range(1, tensor_count):
            peer_copy(j, q).wait_recv()
            total = total + peer[j, q - 1].astype(jnp.float32)
        result = jnp.dot(
            total.astype(jnp.bfloat16), up_wide[slot_ref[j]], preferred_element_type=jnp.float32
        ).astype(jnp.bfloat16)
        if j == 0:
            returned[0] = result
        else:
            served[j - 1] = result
            delta_copy(j).start()

    order = [0]
    for a, b in zip(near, far[: len(near)]):
        order += [a, b]
    order += far[len(near) :]
    behind = None
    for j in order:
        down_stage(j)
        if j != 0:
            waiting = far_waiting if j >= dp_count // 2 else near_waiting
            token_copy(j).wait_send()
            if waiting:
                token_copy(waiting.pop(0)).start()
        if behind is not None:
            up_stage(behind)
        behind = j
    up_stage(behind)
    for j in order:
        if j != 0:
            delta_copy(j).wait_recv()
    for c in range(delta_ref.shape[0]):
        delta_ref[c] = returned[mine_ref[c]]
    for j in range(dp_count):
        if j != 0:
            delta_copy(j).wait_send()
        for q in range(1, tensor_count):
            peer_copy(j, q).wait_send()


def adapter_path(conversation_rows, down, up, pick, slot, mine):
    dp_count, tensor_count = lax.axis_size("dp"), lax.axis_size("tensor")
    conversations, span, width = conversation_rows.shape
    stored, _, double_rank = down.shape
    wide = up.shape[1] * 2 * up.shape[4]
    kind = conversation_rows.dtype
    smem = pl.BlockSpec(memory_space=pltpu.SMEM)
    vmem = pl.BlockSpec(memory_space=pltpu.VMEM)
    return pl.pallas_call(
        functools.partial(adapter_kernel, dp_count, tensor_count),
        out_shape=jax.ShapeDtypeStruct((conversations, span, wide), kind),
        in_specs=[smem, smem, smem, vmem, vmem, vmem],
        out_specs=vmem,
        scratch_shapes=[
            pltpu.VMEM((stored, double_rank, wide), kind),
            pltpu.VMEM((dp_count - 1, span, width), kind),
            pltpu.VMEM((dp_count - 1, span, width), kind),
            pltpu.VMEM((dp_count, span, double_rank), kind),
            pltpu.VMEM((dp_count, tensor_count - 1, span, double_rank), kind),
            pltpu.VMEM((dp_count - 1, span, wide), kind),
            pltpu.VMEM((dp_count, span, wide), kind),
            pltpu.SemaphoreType.DMA((dp_count - 1,)),
            pltpu.SemaphoreType.DMA((dp_count - 1,)),
            pltpu.SemaphoreType.DMA((dp_count, tensor_count - 1)),
            pltpu.SemaphoreType.DMA((dp_count, tensor_count - 1)),
            pltpu.SemaphoreType.DMA((dp_count - 1,)),
            pltpu.SemaphoreType.DMA((dp_count - 1,)),
        ],
        compiler_params=pltpu.CompilerParams(
            collective_id=0, has_side_effects=True, vmem_limit_bytes=40 * 2**20
        ),
        cost_estimate=pl.CostEstimate(
            flops=2 * dp_count * span * width * double_rank,
            bytes_accessed=60_000_000,
            transcendentals=0,
        ),
    )(pick, slot, mine, conversation_rows, down, up)


def body(
    tokens,
    key_value_weight,
    key_value_bias,
    adapter_down_weight,
    adapter_up_weight,
    conversation_adapter,
    adapter_slot_table,
    span_length,
    context_length,
):
    dp_count = lax.axis_size("dp")
    owner_index = lax.axis_index("dp")
    conversation_present = span_length.shape[0]
    span_token_rows = tokens.shape[0] // conversation_present
    slice_width = tokens.shape[1]
    heads_present = key_value_bias.shape[0]
    head_span_width = key_value_bias.shape[1]
    head_dim = head_span_width // 2
    locally_stored = adapter_down_weight.shape[0]
    adapter_ids = jnp.arange(adapter_slot_table.shape[0], dtype=jnp.int32)
    storage = jnp.sum(
        jnp.where(
            conversation_adapter[:, None] == adapter_ids[None, :], adapter_slot_table[None, :], 0
        ),
        axis=1,
    )
    owner_table = (storage // locally_stored).reshape(dp_count, conversation_present)
    local_table = (storage % locally_stored).reshape(dp_count, conversation_present)
    my_owners = lax.dynamic_slice_in_dim(owner_table, owner_index, 1, 0)[0]
    owner_ids = jnp.arange(dp_count, dtype=jnp.int32)
    owner_ids = jnp.arange(dp_count, dtype=jnp.int32)
    partner_ids = owner_index ^ owner_ids
    conversation_ids = jnp.arange(conversation_present, dtype=jnp.int32)
    pick = jnp.sum(
        jnp.where(my_owners[None, :] == partner_ids[:, None], conversation_ids[None, :], 0), axis=1
    )
    served_slot = jnp.sum(jnp.where(owner_table == owner_index, local_table, 0), axis=1)
    slot = jnp.sum(
        jnp.where(partner_ids[:, None] == owner_ids[None, :], served_slot[None, :], 0), axis=1
    )
    mine = my_owners ^ owner_index
    conversation_rows = tokens.reshape(conversation_present, span_token_rows, slice_width)
    base_sum = lax.psum_scatter(
        jnp.einsum(
            "td,dhe->hte", tokens, key_value_weight, preferred_element_type=jnp.float32
        ).astype(jnp.bfloat16),
        "tensor",
        scatter_dimension=0,
        tiled=True,
    ).astype(jnp.float32)
    adapter_delta = adapter_path(
        conversation_rows, adapter_down_weight, adapter_up_weight, pick, slot, mine
    )
    conversation_delta = adapter_delta.reshape(
        conversation_present, span_token_rows, heads_present * head_span_width
    ).astype(jnp.float32)
    delta_heads = jnp.transpose(
        conversation_delta.reshape(
            conversation_present * span_token_rows, heads_present, head_span_width
        ),
        (1, 0, 2),
    )
    projected = base_sum + key_value_bias.astype(jnp.float32)[:, None, :] + delta_heads
    positions = (
        (context_length[:, None] + jnp.arange(span_token_rows, dtype=jnp.int32)[None, :])
        .reshape(-1)
        .astype(jnp.float32)
    )
    rotated = rotary(projected[..., :head_dim], positions)
    live_mask = (
        jnp.arange(span_token_rows, dtype=jnp.int32)[None, :] < span_length[:, None]
    ).reshape(-1)
    joined = jnp.concatenate([rotated, projected[..., head_dim:]], axis=-1)
    return jnp.where(live_mask[None, :, None], joined, 0.0).astype(jnp.bfloat16)


def solution(mesh):
    placed = (
        P("dp", "tensor"),
        P("tensor", None, None),
        P("tensor", None),
        P("dp", "tensor", None),
        P("dp", "tensor", None, None, None),
        P(),
        P(),
        P("dp"),
        P("dp"),
    )
    return jax.shard_map(
        body, mesh=mesh, in_specs=placed, out_specs=P("tensor", "dp", None), check_vma=False
    )
```

```python
import functools
import math

import jax
import jax.numpy as jnp
from jax import lax
from jax.experimental import pallas as pl
from jax.experimental.pallas import tpu as pltpu
from jax.sharding import PartitionSpec as P

rope_base = 1000000.0


def rotary_tables(positions, head_dim):
    half_dim = head_dim // 2
    inverse_freq = jnp.exp(
        jnp.arange(half_dim, dtype=jnp.float32) * (-2.0 * math.log(rope_base) / head_dim)
    )
    angles = positions[:, None] * inverse_freq[None, :]
    cosines, sines = jnp.cos(angles), jnp.sin(angles)
    return (
        jnp.concatenate([cosines, cosines], axis=-1),
        jnp.concatenate([-sines, sines], axis=-1),
    )


def other(index, distance, count):
    total = 0
    step = 1
    while step < count:
        bit = lax.rem(index // step, 2)
        total = total + (bit if (distance // step) % 2 == 0 else 1 - bit) * step
        step *= 2
    return total


def projection_kernel(
    dp_count,
    tensor_count,
    pick_ref,
    slot_ref,
    mine_ref,
    tokens_ref,
    down_ref,
    up_ref,
    weight_ref,
    bias_ref,
    cos_ref,
    sin_ref,
    live_ref,
    result_ref,
    raw_weight,
    head_weight,
    base_part,
    base_peer,
    base_total,
    up_wide,
    outgoing,
    visiting,
    part,
    peer,
    served,
    returned,
    token_send,
    token_recv,
    peer_send,
    peer_recv,
    delta_send,
    delta_recv,
    weight_sem,
    base_send,
    base_recv,
):
    me_dp = lax.axis_index("dp")
    me_tensor = lax.axis_index("tensor")
    stored, heads = up_ref.shape[0], up_ref.shape[1]
    rank, half = up_ref.shape[3], up_ref.shape[4]
    partner = [other(me_dp, j, dp_count) for j in range(dp_count)]
    mate = [other(me_tensor, q, tensor_count) for q in range(tensor_count)]

    chunks = weight_sem.shape[0]
    chunk = weight_ref.shape[0] // chunks
    conversations, span = tokens_ref.shape[0], tokens_ref.shape[1]
    width = tokens_ref.shape[2]

    def weight_copy(n):
        return pltpu.make_async_copy(
            weight_ref.at[pl.ds(n * chunk, chunk)],
            raw_weight.at[pl.ds(n * chunk, chunk)],
            weight_sem.at[n],
        )

    for n in range(chunks):
        weight_copy(n).start()

    barrier = pltpu.get_barrier_semaphore()
    for j in range(1, dp_count):
        pl.semaphore_signal(
            barrier, inc=1, device_id={"dp": partner[j]}, device_id_type=pl.DeviceIdType.MESH
        )
    for q in range(1, tensor_count):
        pl.semaphore_signal(
            barrier, inc=1, device_id={"tensor": mate[q]}, device_id_type=pl.DeviceIdType.MESH
        )

    def token_copy(j):
        return pltpu.make_async_remote_copy(
            src_ref=outgoing.at[j - 1],
            dst_ref=visiting.at[j - 1],
            send_sem=token_send.at[j - 1],
            recv_sem=token_recv.at[j - 1],
            device_id={"dp": partner[j]},
            device_id_type=pl.DeviceIdType.MESH,
        )

    def peer_copy(j, q):
        return pltpu.make_async_remote_copy(
            src_ref=part.at[j],
            dst_ref=peer.at[j, q - 1],
            send_sem=peer_send.at[j, q - 1],
            recv_sem=peer_recv.at[j, q - 1],
            device_id={"tensor": mate[q]},
            device_id_type=pl.DeviceIdType.MESH,
        )

    def delta_copy(j):
        return pltpu.make_async_remote_copy(
            src_ref=served.at[j - 1],
            dst_ref=returned.at[j],
            send_sem=delta_send.at[j - 1],
            recv_sem=delta_recv.at[j - 1],
            device_id={"dp": partner[j]},
            device_id_type=pl.DeviceIdType.MESH,
        )

    def base_copy(q):
        return pltpu.make_async_remote_copy(
            src_ref=base_part.at[q],
            dst_ref=base_peer.at[q - 1],
            send_sem=base_send.at[q - 1],
            recv_sem=base_recv.at[q - 1],
            device_id={"tensor": mate[q]},
            device_id_type=pl.DeviceIdType.MESH,
        )

    def turn_weight(n):
        weight_copy(n).wait()
        block = raw_weight[n * chunk : (n + 1) * chunk]
        for h in range(block.shape[1]):
            head_weight[h, n * chunk : (n + 1) * chunk] = block[:, h, :]

    def base_stage(q):
        rows = tokens_ref[...].reshape(conversations * span, width)
        for h in range(heads):
            base_part[q, h] = jnp.dot(
                rows, head_weight[mate[q] * heads + h], preferred_element_type=jnp.float32
            ).astype(jnp.bfloat16)
        if q != 0:
            base_copy(q).start()

    def base_finish():
        for q in range(1, tensor_count):
            base_copy(q).wait_recv()
        for h in range(heads):
            total = base_part[0, h].astype(jnp.float32)
            for q in range(1, tensor_count):
                total = total + base_peer[q - 1, h].astype(jnp.float32)
            base_total[h] = total + bias_ref[h : h + 1, :].astype(jnp.float32)

    def fill(j):
        outgoing[j - 1] = tokens_ref[pick_ref[j]]

    far = list(range(dp_count - 1, dp_count // 2 - 1, -1))
    near = list(range(dp_count // 2 - 1, 0, -1))
    first = [far[0], near[0], far[1], near[1], far[2]]
    for j in first:
        fill(j)
    pl.semaphore_wait(barrier, dp_count + tensor_count - 2)
    for j in first:
        token_copy(j).start()
    far_waiting, near_waiting = far[3:], near[2:]
    for j in far_waiting + near_waiting:
        fill(j)

    up_wide[...] = jnp.zeros_like(up_wide)
    for s in range(stored):
        for h in range(heads):
            for g in range(2):
                at = (2 * h + g) * half
                up_wide[s, g * rank : (g + 1) * rank, at : at + half] = up_ref[s, h, g]

    def down_stage(j):
        if j == 0:
            rows = tokens_ref[pick_ref[0]]
        else:
            token_copy(j).wait_recv()
            rows = visiting[j - 1]
        part[j] = jnp.dot(
            rows, down_ref[slot_ref[j]], preferred_element_type=jnp.float32
        ).astype(jnp.bfloat16)
        for q in range(1, tensor_count):
            peer_copy(j, q).start()

    def up_stage(j):
        total = part[j].astype(jnp.float32)
        for q in range(1, tensor_count):
            peer_copy(j, q).wait_recv()
            total = total + peer[j, q - 1].astype(jnp.float32)
        result = jnp.dot(
            total.astype(jnp.bfloat16), up_wide[slot_ref[j]], preferred_element_type=jnp.float32
        ).astype(jnp.bfloat16)
        if j == 0:
            returned[0] = result
        else:
            served[j - 1] = result
            delta_copy(j).start()

    order = [0]
    for a, b in zip(near, far[: len(near)]):
        order += [a, b]
    order += far[len(near) :]
    down_stage(0)
    for n in range(chunks):
        turn_weight(n)
    base_stages = list(range(1, tensor_count)) + [0]
    base_stages = [base_stages[n::3] for n in range(3)]
    order = order[1:]
    behind = 0
    for n, j in enumerate(order):
        down_stage(j)
        if j != 0:
            waiting = far_waiting if j >= dp_count // 2 else near_waiting
            token_copy(j).wait_send()
            if waiting:
                token_copy(waiting.pop(0)).start()
        if n < 3:
            for q in base_stages[n]:
                base_stage(q)
        up_stage(behind)
        if n == 4:
            base_finish()
        behind = j
    up_stage(behind)
    for j in order:
        delta_copy(j).wait_recv()
    for c in range(conversations):
        delta = returned[mine_ref[c]].astype(jnp.float32)
        at = slice(c * span, (c + 1) * span)
        for h in range(heads):
            whole = base_total[h, at, :] + delta[:, 2 * half * h : 2 * half * (h + 1)]
            key_part, value_part = whole[:, :half], whole[:, half:]
            turned = pltpu.roll(key_part, half // 2, 1)
            key_part = key_part * cos_ref[at, :] + turned * sin_ref[at, :]
            live = live_ref[at, :] > 0.5
            result_ref[h, at, :half] = jnp.where(live, key_part, 0.0).astype(jnp.bfloat16)
            result_ref[h, at, half:] = jnp.where(live, value_part, 0.0).astype(jnp.bfloat16)
    for j in range(dp_count):
        if j != 0:
            delta_copy(j).wait_send()
        for q in range(1, tensor_count):
            peer_copy(j, q).wait_send()
    for q in range(1, tensor_count):
        base_copy(q).wait_send()


def project(conversation_rows, down, up, weight, bias, cosines, sines, live, pick, slot, mine):
    dp_count, tensor_count = lax.axis_size("dp"), lax.axis_size("tensor")
    conversations, span, width = conversation_rows.shape
    stored, _, double_rank = down.shape
    wide = up.shape[1] * 2 * up.shape[4]
    kind = conversation_rows.dtype
    heads, head_width = bias.shape
    rows = conversations * span
    chunks = 8
    smem = pl.BlockSpec(memory_space=pltpu.SMEM)
    vmem = pl.BlockSpec(memory_space=pltpu.VMEM)
    return pl.pallas_call(
        functools.partial(projection_kernel, dp_count, tensor_count),
        out_shape=jax.ShapeDtypeStruct((heads, rows, head_width), kind),
        in_specs=[smem] * 3 + [vmem] * 3 + [pl.BlockSpec(memory_space=pl.ANY)] + [vmem] * 4,
        out_specs=vmem,
        scratch_shapes=[
            pltpu.VMEM(weight.shape, kind),
            pltpu.VMEM((weight.shape[1], width, head_width), kind),
            pltpu.VMEM((tensor_count, heads, rows, head_width), kind),
            pltpu.VMEM((tensor_count - 1, heads, rows, head_width), kind),
            pltpu.VMEM((heads, rows, head_width), jnp.float32),
            pltpu.VMEM((stored, double_rank, wide), kind),
            pltpu.VMEM((dp_count - 1, span, width), kind),
            pltpu.VMEM((dp_count - 1, span, width), kind),
            pltpu.VMEM((dp_count, span, double_rank), kind),
            pltpu.VMEM((dp_count, tensor_count - 1, span, double_rank), kind),
            pltpu.VMEM((dp_count - 1, span, wide), kind),
            pltpu.VMEM((dp_count, span, wide), kind),
            pltpu.SemaphoreType.DMA((dp_count - 1,)),
            pltpu.SemaphoreType.DMA((dp_count - 1,)),
            pltpu.SemaphoreType.DMA((dp_count, tensor_count - 1)),
            pltpu.SemaphoreType.DMA((dp_count, tensor_count - 1)),
            pltpu.SemaphoreType.DMA((dp_count - 1,)),
            pltpu.SemaphoreType.DMA((dp_count - 1,)),
            pltpu.SemaphoreType.DMA((chunks,)),
            pltpu.SemaphoreType.DMA((tensor_count - 1,)),
            pltpu.SemaphoreType.DMA((tensor_count - 1,)),
        ],
        compiler_params=pltpu.CompilerParams(
            collective_id=0, has_side_effects=True, vmem_limit_bytes=52 * 2**20
        ),
        cost_estimate=pl.CostEstimate(
            flops=2 * dp_count * span * width * double_rank,
            bytes_accessed=60_000_000,
            transcendentals=0,
        ),
    )(pick, slot, mine, conversation_rows, down, up, weight, bias, cosines, sines, live)


def body(
    tokens,
    key_value_weight,
    key_value_bias,
    adapter_down_weight,
    adapter_up_weight,
    conversation_adapter,
    adapter_slot_table,
    span_length,
    context_length,
):
    dp_count = lax.axis_size("dp")
    owner_index = lax.axis_index("dp")
    conversation_present = span_length.shape[0]
    span_token_rows = tokens.shape[0] // conversation_present
    slice_width = tokens.shape[1]
    head_span_width = key_value_bias.shape[1]
    head_dim = head_span_width // 2
    locally_stored = adapter_down_weight.shape[0]
    adapter_ids = jnp.arange(adapter_slot_table.shape[0], dtype=jnp.int32)
    storage = jnp.sum(
        jnp.where(
            conversation_adapter[:, None] == adapter_ids[None, :], adapter_slot_table[None, :], 0
        ),
        axis=1,
    )
    owner_table = (storage // locally_stored).reshape(dp_count, conversation_present)
    local_table = (storage % locally_stored).reshape(dp_count, conversation_present)
    my_owners = lax.dynamic_slice_in_dim(owner_table, owner_index, 1, 0)[0]
    owner_ids = jnp.arange(dp_count, dtype=jnp.int32)
    owner_ids = jnp.arange(dp_count, dtype=jnp.int32)
    partner_ids = owner_index ^ owner_ids
    conversation_ids = jnp.arange(conversation_present, dtype=jnp.int32)
    pick = jnp.sum(
        jnp.where(my_owners[None, :] == partner_ids[:, None], conversation_ids[None, :], 0), axis=1
    )
    served_slot = jnp.sum(jnp.where(owner_table == owner_index, local_table, 0), axis=1)
    slot = jnp.sum(
        jnp.where(partner_ids[:, None] == owner_ids[None, :], served_slot[None, :], 0), axis=1
    )
    mine = my_owners ^ owner_index
    conversation_rows = tokens.reshape(conversation_present, span_token_rows, slice_width)
    positions = (
        (context_length[:, None] + jnp.arange(span_token_rows, dtype=jnp.int32)[None, :])
        .reshape(-1)
        .astype(jnp.float32)
    )
    cosines, sines = rotary_tables(positions, head_dim)
    live_mask = (
        jnp.arange(span_token_rows, dtype=jnp.int32)[None, :] < span_length[:, None]
    ).reshape(-1)
    live = jnp.broadcast_to(
        live_mask[:, None].astype(jnp.float32), (live_mask.shape[0], head_dim)
    )
    return project(
        conversation_rows,
        adapter_down_weight,
        adapter_up_weight,
        key_value_weight,
        key_value_bias,
        cosines,
        sines,
        live,
        pick,
        slot,
        mine,
    )


def solution(mesh):
    placed = (
        P("dp", "tensor"),
        P("tensor", None, None),
        P("tensor", None),
        P("dp", "tensor", None),
        P("dp", "tensor", None, None, None),
        P(),
        P(),
        P("dp"),
        P("dp"),
    )
    return jax.shard_map(
        body, mesh=mesh, in_specs=placed, out_specs=P("tensor", "dp", None), check_vma=False
    )
```

```python
import functools
import math

import jax
import jax.numpy as jnp
from jax import lax
from jax.experimental import pallas as pl
from jax.experimental.pallas import tpu as pltpu
from jax.sharding import PartitionSpec as P

rope_base = 1000000.0


def rotary_tables(positions, head_dim):
    half_dim = head_dim // 2
    inverse_freq = jnp.exp(
        jnp.arange(half_dim, dtype=jnp.float32) * (-2.0 * math.log(rope_base) / head_dim)
    )
    angles = positions[:, None] * inverse_freq[None, :]
    cosines, sines = jnp.cos(angles), jnp.sin(angles)
    return (
        jnp.concatenate([cosines, cosines], axis=-1),
        jnp.concatenate([-sines, sines], axis=-1),
    )


def other(index, distance, count):
    total = 0
    step = 1
    while step < count:
        bit = lax.rem(index // step, 2)
        total = total + (bit if (distance // step) % 2 == 0 else 1 - bit) * step
        step *= 2
    return total


def projection_kernel(
    dp_count,
    tensor_count,
    pick_ref,
    slot_ref,
    mine_ref,
    home_ref,
    tokens_ref,
    stored_down,
    up_ref,
    weight_ref,
    bias_ref,
    cos_ref,
    sin_ref,
    live_ref,
    result_ref,
    raw_weight,
    head_weight,
    base_part,
    base_peer,
    base_total,
    down_ref,
    up_wide,
    up_all,
    outgoing,
    visiting,
    part,
    peer,
    served,
    returned,
    token_send,
    token_recv,
    peer_send,
    peer_recv,
    rank_send,
    rank_recv,
    weight_sem,
    base_send,
    base_recv,
    up_send,
    up_recv,
    down_sem,
):
    me_dp = lax.axis_index("dp")
    me_tensor = lax.axis_index("tensor")
    heads = up_ref.shape[1]
    across = dp_count // 2
    rank, half = up_ref.shape[3], up_ref.shape[4]
    partner = [other(me_dp, j, dp_count) for j in range(dp_count)]
    mate = [other(me_tensor, q, tensor_count) for q in range(tensor_count)]

    chunks = weight_sem.shape[0]
    chunk = weight_ref.shape[0] // chunks
    conversations, span = tokens_ref.shape[0], tokens_ref.shape[1]
    width = tokens_ref.shape[2]

    def weight_copy(n):
        return pltpu.make_async_copy(
            weight_ref.at[pl.ds(n * chunk, chunk)],
            raw_weight.at[pl.ds(n * chunk, chunk)],
            weight_sem.at[n],
        )

    down_fetch = pltpu.make_async_copy(stored_down, down_ref, down_sem)
    down_fetch.start()
    for n in range(chunks):
        weight_copy(n).start()

    barrier = pltpu.get_barrier_semaphore()
    for j in range(1, dp_count):
        pl.semaphore_signal(
            barrier, inc=1, device_id={"dp": partner[j]}, device_id_type=pl.DeviceIdType.MESH
        )
    for q in range(1, tensor_count):
        pl.semaphore_signal(
            barrier, inc=1, device_id={"tensor": mate[q]}, device_id_type=pl.DeviceIdType.MESH
        )

    def token_copy(j):
        return pltpu.make_async_remote_copy(
            src_ref=outgoing.at[j - 1],
            dst_ref=visiting.at[j - 1],
            send_sem=token_send.at[j - 1],
            recv_sem=token_recv.at[j - 1],
            device_id={"dp": partner[j]},
            device_id_type=pl.DeviceIdType.MESH,
        )

    def peer_copy(j, q):
        return pltpu.make_async_remote_copy(
            src_ref=part.at[j],
            dst_ref=peer.at[j, q - 1],
            send_sem=peer_send.at[j, q - 1],
            recv_sem=peer_recv.at[j, q - 1],
            device_id={"tensor": mate[q]},
            device_id_type=pl.DeviceIdType.MESH,
        )

    def up_copy(source, j, to):
        return pltpu.make_async_remote_copy(
            src_ref=source,
            dst_ref=up_all.at[j],
            send_sem=up_send.at[j - 1],
            recv_sem=up_recv.at[j - 1],
            device_id={"dp": partner[to]},
            device_id_type=pl.DeviceIdType.MESH,
        )

    def up_direct(j):
        return up_copy(up_ref, j, j)

    def up_relay(j):
        return up_copy(up_all.at[across], across + j, j)

    def rank_copy(j):
        return pltpu.make_async_remote_copy(
            src_ref=served.at[j - 1],
            dst_ref=returned.at[j],
            send_sem=rank_send.at[j - 1],
            recv_sem=rank_recv.at[j - 1],
            device_id={"dp": partner[j]},
            device_id_type=pl.DeviceIdType.MESH,
        )

    def base_copy(q):
        return pltpu.make_async_remote_copy(
            src_ref=base_part.at[q],
            dst_ref=base_peer.at[q - 1],
            send_sem=base_send.at[q - 1],
            recv_sem=base_recv.at[q - 1],
            device_id={"tensor": mate[q]},
            device_id_type=pl.DeviceIdType.MESH,
        )

    def turn_weight(n):
        weight_copy(n).wait()
        block = raw_weight[n * chunk : (n + 1) * chunk]
        for h in range(block.shape[1]):
            head_weight[h, n * chunk : (n + 1) * chunk] = block[:, h, :]

    def base_stage(q):
        rows = tokens_ref[...].reshape(conversations * span, width)
        for h in range(heads):
            base_part[q, h] = jnp.dot(
                rows, head_weight[mate[q] * heads + h], preferred_element_type=jnp.float32
            ).astype(jnp.bfloat16)
        if q != 0:
            base_copy(q).start()

    def base_finish():
        for q in range(1, tensor_count):
            base_copy(q).wait_recv()
        for h in range(heads):
            total = base_part[0, h].astype(jnp.float32)
            for q in range(1, tensor_count):
                total = total + base_peer[q - 1, h].astype(jnp.float32)
            base_total[h] = total + bias_ref[h : h + 1, :].astype(jnp.float32)

    def fill(j):
        outgoing[j - 1] = tokens_ref[pick_ref[j]]

    far = list(range(dp_count - 1, dp_count // 2 - 1, -1))
    near = list(range(dp_count // 2 - 1, 0, -1))
    first = [far[0], near[0], far[1], near[1], far[2]]
    for j in first:
        fill(j)
    pl.semaphore_wait(barrier, dp_count + tensor_count - 2)
    for j in first:
        token_copy(j).start()
    far_waiting, near_waiting = far[3:], near[2:]
    for j in far_waiting + near_waiting:
        fill(j)

    for j in [across] + list(range(1, across)):
        up_direct(j).start()
    up_all[0] = up_ref[...]
    up_wide[...] = jnp.zeros_like(up_wide)

    def relay_up():
        up_direct(across).wait_recv()
        for j in range(1, across):
            up_relay(j).start()

    def widen_up():
        for j in range(1, across):
            up_direct(j).wait_recv()
            up_relay(j).wait_recv()
        for c in range(conversations):
            for h in range(heads):
                for g in range(2):
                    at = (2 * h + g) * half
                    up_wide[c, g * rank : (g + 1) * rank, at : at + half] = up_all[
                        mine_ref[c], home_ref[c], h, g
                    ]

    def down_stage(j):
        if j == 0:
            rows = tokens_ref[pick_ref[0]]
        else:
            token_copy(j).wait_recv()
            rows = visiting[j - 1]
        part[j] = jnp.dot(
            rows, down_ref[slot_ref[j]], preferred_element_type=jnp.float32
        ).astype(jnp.bfloat16)
        for q in range(1, tensor_count):
            peer_copy(j, q).start()

    def sum_stage(j):
        total = part[j].astype(jnp.float32)
        for q in range(1, tensor_count):
            peer_copy(j, q).wait_recv()
            total = total + peer[j, q - 1].astype(jnp.float32)
        result = total.astype(jnp.bfloat16)
        if j == 0:
            returned[0] = result
        else:
            served[j - 1] = result
            rank_copy(j).start()

    order = [0]
    for a, b in zip(near, far[: len(near)]):
        order += [a, b]
    order += far[len(near) :]
    down_fetch.wait()
    down_stage(0)
    for n in range(chunks):
        turn_weight(n)
    base_stages = list(range(1, tensor_count)) + [0]
    base_stages = [base_stages[n::3] for n in range(3)]
    order = order[1:]
    behind = 0
    for n, j in enumerate(order):
        down_stage(j)
        if j != 0:
            waiting = far_waiting if j >= dp_count // 2 else near_waiting
            token_copy(j).wait_send()
            if waiting:
                token_copy(waiting.pop(0)).start()
        if n < 3:
            for q in base_stages[n]:
                base_stage(q)
        sum_stage(behind)
        if n == 1:
            relay_up()
        if n == 4:
            base_finish()
        if n == 5:
            widen_up()
        behind = j
    sum_stage(behind)
    for j in order:
        rank_copy(j).wait_recv()
    for c in range(conversations):
        delta = jnp.dot(
            returned[mine_ref[c]], up_wide[c], preferred_element_type=jnp.float32
        )
        delta = delta.astype(jnp.bfloat16).astype(jnp.float32)
        at = slice(c * span, (c + 1) * span)
        for h in range(heads):
            whole = base_total[h, at, :] + delta[:, 2 * half * h : 2 * half * (h + 1)]
            key_part, value_part = whole[:, :half], whole[:, half:]
            turned = pltpu.roll(key_part, half // 2, 1)
            key_part = key_part * cos_ref[at, :] + turned * sin_ref[at, :]
            live = live_ref[at, :] > 0.5
            result_ref[h, at, :half] = jnp.where(live, key_part, 0.0).astype(jnp.bfloat16)
            result_ref[h, at, half:] = jnp.where(live, value_part, 0.0).astype(jnp.bfloat16)
    for j in range(dp_count):
        if j != 0:
            rank_copy(j).wait_send()
        for q in range(1, tensor_count):
            peer_copy(j, q).wait_send()
    for q in range(1, tensor_count):
        base_copy(q).wait_send()
    for j in range(1, across + 1):
        up_direct(j).wait_send()
    for j in range(1, across):
        up_relay(j).wait_send()


def project(conversation_rows, down, up, weight, bias, cosines, sines, live, pick, slot, mine, home):
    dp_count, tensor_count = lax.axis_size("dp"), lax.axis_size("tensor")
    conversations, span, width = conversation_rows.shape
    double_rank = down.shape[2]
    wide = up.shape[1] * 2 * up.shape[4]
    kind = conversation_rows.dtype
    heads, head_width = bias.shape
    rows = conversations * span
    chunks = 8
    smem = pl.BlockSpec(memory_space=pltpu.SMEM)
    vmem = pl.BlockSpec(memory_space=pltpu.VMEM)
    hbm = pl.BlockSpec(memory_space=pl.ANY)
    return pl.pallas_call(
        functools.partial(projection_kernel, dp_count, tensor_count),
        out_shape=jax.ShapeDtypeStruct((heads, rows, head_width), kind),
        in_specs=[smem] * 4 + [vmem, hbm, vmem, hbm] + [vmem] * 4,
        out_specs=vmem,
        scratch_shapes=[
            pltpu.VMEM(weight.shape, kind),
            pltpu.VMEM((weight.shape[1], width, head_width), kind),
            pltpu.VMEM((tensor_count, heads, rows, head_width), kind),
            pltpu.VMEM((tensor_count - 1, heads, rows, head_width), kind),
            pltpu.VMEM((heads, rows, head_width), jnp.float32),
            pltpu.VMEM(down.shape, kind),
            pltpu.VMEM((conversations, double_rank, wide), kind),
            pltpu.VMEM((dp_count,) + up.shape, kind),
            pltpu.VMEM((dp_count - 1, span, width), kind),
            pltpu.VMEM((dp_count - 1, span, width), kind),
            pltpu.VMEM((dp_count, span, double_rank), kind),
            pltpu.VMEM((dp_count, tensor_count - 1, span, double_rank), kind),
            pltpu.VMEM((dp_count - 1, span, double_rank), kind),
            pltpu.VMEM((dp_count, span, double_rank), kind),
            pltpu.SemaphoreType.DMA((dp_count - 1,)),
            pltpu.SemaphoreType.DMA((dp_count - 1,)),
            pltpu.SemaphoreType.DMA((dp_count, tensor_count - 1)),
            pltpu.SemaphoreType.DMA((dp_count, tensor_count - 1)),
            pltpu.SemaphoreType.DMA((dp_count - 1,)),
            pltpu.SemaphoreType.DMA((dp_count - 1,)),
            pltpu.SemaphoreType.DMA((chunks,)),
            pltpu.SemaphoreType.DMA((tensor_count - 1,)),
            pltpu.SemaphoreType.DMA((tensor_count - 1,)),
            pltpu.SemaphoreType.DMA((dp_count - 1,)),
            pltpu.SemaphoreType.DMA((dp_count - 1,)),
            pltpu.SemaphoreType.DMA,
        ],
        compiler_params=pltpu.CompilerParams(
            collective_id=0, has_side_effects=True, vmem_limit_bytes=52 * 2**20
        ),
        cost_estimate=pl.CostEstimate(
            flops=2 * dp_count * span * width * double_rank,
            bytes_accessed=60_000_000,
            transcendentals=0,
        ),
    )(pick, slot, mine, home, conversation_rows, down, up, weight, bias, cosines, sines, live)


def body(
    tokens,
    key_value_weight,
    key_value_bias,
    adapter_down_weight,
    adapter_up_weight,
    conversation_adapter,
    adapter_slot_table,
    span_length,
    context_length,
):
    dp_count = lax.axis_size("dp")
    owner_index = lax.axis_index("dp")
    conversation_present = span_length.shape[0]
    span_token_rows = tokens.shape[0] // conversation_present
    slice_width = tokens.shape[1]
    head_span_width = key_value_bias.shape[1]
    head_dim = head_span_width // 2
    locally_stored = adapter_down_weight.shape[0]
    adapter_ids = jnp.arange(adapter_slot_table.shape[0], dtype=jnp.int32)
    storage = jnp.sum(
        jnp.where(
            conversation_adapter[:, None] == adapter_ids[None, :], adapter_slot_table[None, :], 0
        ),
        axis=1,
    )
    owner_table = (storage // locally_stored).reshape(dp_count, conversation_present)
    local_table = (storage % locally_stored).reshape(dp_count, conversation_present)
    my_owners = lax.dynamic_slice_in_dim(owner_table, owner_index, 1, 0)[0]
    owner_ids = jnp.arange(dp_count, dtype=jnp.int32)
    owner_ids = jnp.arange(dp_count, dtype=jnp.int32)
    partner_ids = owner_index ^ owner_ids
    conversation_ids = jnp.arange(conversation_present, dtype=jnp.int32)
    pick = jnp.sum(
        jnp.where(my_owners[None, :] == partner_ids[:, None], conversation_ids[None, :], 0), axis=1
    )
    served_slot = jnp.sum(jnp.where(owner_table == owner_index, local_table, 0), axis=1)
    slot = jnp.sum(
        jnp.where(partner_ids[:, None] == owner_ids[None, :], served_slot[None, :], 0), axis=1
    )
    mine = my_owners ^ owner_index
    home = lax.dynamic_slice_in_dim(local_table, owner_index, 1, 0)[0]
    conversation_rows = tokens.reshape(conversation_present, span_token_rows, slice_width)
    positions = (
        (context_length[:, None] + jnp.arange(span_token_rows, dtype=jnp.int32)[None, :])
        .reshape(-1)
        .astype(jnp.float32)
    )
    cosines, sines = rotary_tables(positions, head_dim)
    live_mask = (
        jnp.arange(span_token_rows, dtype=jnp.int32)[None, :] < span_length[:, None]
    ).reshape(-1)
    live = jnp.broadcast_to(
        live_mask[:, None].astype(jnp.float32), (live_mask.shape[0], head_dim)
    )
    return project(
        conversation_rows,
        adapter_down_weight,
        adapter_up_weight,
        key_value_weight,
        key_value_bias,
        cosines,
        sines,
        live,
        pick,
        slot,
        mine,
        home,
    )


def solution(mesh):
    placed = (
        P("dp", "tensor"),
        P("tensor", None, None),
        P("tensor", None),
        P("dp", "tensor", None),
        P("dp", "tensor", None, None, None),
        P(),
        P(),
        P("dp"),
        P("dp"),
    )
    return jax.shard_map(
        body, mesh=mesh, in_specs=placed, out_specs=P("tensor", "dp", None), check_vma=False
    )
```
